32 devices in a mesh: dom: 2 (over y), rep: 4 (over z), tp: 4 (over x, core).
Axes of the slice: x: 2, y: 2, z: 4, core: 2. Of those that a mesh axis runs over, the one named last changes fastest.
Arguments:
- normed_hidden: bfloat16 [4, 1536, 8192], P(None, ('dom', 'rep'), 'tp'), parts along dimension 1, may hold values from -6 to 6
- key_weight_base: bfloat16 [8192, 1024], P('tp'), may hold values from -0.0625 to 0.0625
- adapter_down_factors: bfloat16 [256, 64, 8192], P('rep', None, 'tp'), may hold values from -0.0625 to 0.0625
- adapter_up_factors: bfloat16 [256, 64, 1024], P('rep', None, 'tp'), may hold values from -0.75 to 0.75
- request_adapter: int32 [1536], P(('dom', 'rep')), parts along dimension 0, may hold values from 0 to 255, as said below
- adapter_position: int32 [512], P('dom'), parts along dimension 0, may hold values from 0 to 255, as said below
Outputs:
- keys: bfloat16 [4, 1536, 1024], P(None, ('dom', 'rep'), 'tp'), parts along dimension 1
The draws below stay inside these ranges and needn't reach their ends.
There are 2 independent parts, one for each index of `dom`. The reference program is written for one: setup_inputs(seed, part) draws one part's arguments, and reference() takes and returns one part's arrays. A program takes and returns all parts, laid end to end along the dimension named above; an argument that names none is the same for every part. Nothing has to cross between parts.
Inputs may be any that keep to these rules, and one draw needn't show every extreme that they name: `adapter_position`: A permutation; the factors of storage position p lie on the replica of index p // (256 // 4). `request_adapter`: among the 192 requests of one replica, at most 96 use adapters stored on any one replica.
All inputs are finite; a program needn't handle non-finite values.
Results may differ from the reference program's by a relative error of at most 0.001.
Values may be sent and summed in bfloat16 or wider, within the bound.
A program may use at most 128 MiB of HBM per device.

```python
import jax
import jax.numpy as jnp
from jax import lax

MODEL_WIDTH = 8192
KEY_FEATURES = 1024
ADAPTER_RANK = 64
ADAPTER_TOTAL = 256
STEPS = 4
REQ_DEV = 192
REQUESTS = 768
N_REP = 4


def storage_order(key):
    return jax.random.permutation(key, ADAPTER_TOTAL).astype(jnp.int32)


def draw_adapter_position(key, part):
    order = storage_order(key)
    return order


def draw_request_adapter(key, part):
    order = storage_order(key)
    key = jax.random.fold_in(key, 11)
    owner_grouped = ADAPTER_TOTAL // N_REP
    capacity = 2 * REQ_DEV // N_REP
    total_slots = N_REP * capacity
    inverse = jnp.argsort(order).astype(jnp.int32)
    busiest = jax.random.randint(jax.random.fold_in(key, 1), (), 0, N_REP)

    def one_block(block_key):
        keys = jax.random.split(block_key, 3)
        counter = jnp.arange(total_slots, dtype=jnp.int32)
        owners_all = counter // capacity
        scores = jax.random.randint(keys[0], (total_slots,), 0, 1 << 20) * total_slots + counter
        scores = jnp.where(owners_all == busiest, counter - total_slots, scores)
        chosen = owners_all[jnp.argsort(scores, stable=True)[:REQ_DEV]]
        chosen = jax.random.permutation(keys[1], chosen)
        offset = jax.random.randint(keys[2], (REQ_DEV,), 0, owner_grouped)
        return inverse[chosen * owner_grouped + offset]
    block_keys = jax.random.split(jax.random.fold_in(key, 2), N_REP)
    return jax.vmap(one_block)(block_keys).reshape(-1).astype(jnp.int32)


def block_levels(stream_key, shape, cuts, least, top_value):
    loudness = 1.0
    for dim, blocks in cuts:
        draws = jax.random.uniform(jax.random.fold_in(jax.random.fold_in(stream_key, 6), dim), (blocks,), jnp.float32, least / len(cuts), top_value / len(cuts))
        loudness = loudness * jnp.repeat(jnp.exp(draws), shape[dim] // blocks).reshape((-1,) + (1,) * (len(shape) - 1 - dim))
    return loudness


def noise(key, shape, width, bound, pieces=(), kind=jnp.bfloat16):
    entries = width * jax.random.normal(key, shape, jnp.float32)
    if pieces:
        entries = entries * block_levels(key, shape, pieces, -0.22, 0.18)
    return jnp.clip(entries, -bound, bound).astype(kind)


def setup_inputs(seed: int = 0, part: int = 0) -> dict:
    seeds = jax.random.split(jax.random.key(seed), 7)
    part_splits = jax.random.split(jax.random.fold_in(seeds[6], part), 7)
    normed_hidden = noise(part_splits[0], (STEPS, REQUESTS, MODEL_WIDTH), 1.0, 6.0, ((1, 4), (2, 4)))
    key_weight_base = noise(seeds[1], (MODEL_WIDTH, KEY_FEATURES), MODEL_WIDTH ** -0.5, 0.0625, ((0, 4),))
    adapter_down_factors = noise(seeds[2], (ADAPTER_TOTAL, ADAPTER_RANK, MODEL_WIDTH), MODEL_WIDTH ** -0.5, 0.0625, ((0, 4), (2, 4)))
    adapter_up_factors = noise(seeds[3], (ADAPTER_TOTAL, ADAPTER_RANK, KEY_FEATURES), ADAPTER_RANK ** -0.5, 0.75, ((0, 4), (2, 4)))
    request_adapter = draw_request_adapter(jax.random.fold_in(jax.random.fold_in(seeds[6], part), 71), part)
    adapter_position = draw_adapter_position(jax.random.fold_in(jax.random.fold_in(seeds[6], part), 71), part)
    return dict(normed_hidden=normed_hidden, key_weight_base=key_weight_base, adapter_down_factors=adapter_down_factors, adapter_up_factors=adapter_up_factors, request_adapter=request_adapter, adapter_position=adapter_position)


def reference(normed_hidden, key_weight_base, adapter_down_factors, adapter_up_factors, request_adapter, adapter_position):
    flat = normed_hidden.reshape(-1, MODEL_WIDTH)
    base_part = jnp.dot(flat, key_weight_base, preferred_element_type=jnp.float32).reshape(STEPS, REQUESTS, KEY_FEATURES)
    position = adapter_position[request_adapter].astype(jnp.int32)
    block_count = REQUESTS // REQ_DEV
    block_grouped = normed_hidden.reshape(STEPS, block_count, REQ_DEV, MODEL_WIDTH).transpose(1, 0, 2, 3)
    storage_places = position.reshape(block_count, REQ_DEV)

    def adapter_block(index_pairing):
        inputs, request_row_locations = index_pairing
        down_factor_rows = adapter_down_factors[request_row_locations].astype(jnp.float32)
        shrink = jnp.einsum("srd,rkd->srk", inputs.astype(jnp.float32), down_factor_rows, precision=lax.Precision.HIGHEST)
        up_factor_rows = adapter_up_factors[request_row_locations].astype(jnp.float32)
        return jnp.einsum("srk,rkc->src", shrink, up_factor_rows, precision=lax.Precision.HIGHEST)

    key_deltas = lax.map(adapter_block, (block_grouped, storage_places))
    key_deltas = key_deltas.transpose(1, 0, 2, 3).reshape(STEPS, REQUESTS, KEY_FEATURES)
    return (base_part + key_deltas).astype(jnp.bfloat16)
```

```python
import functools

import jax
import jax.numpy as jnp
from jax import lax
from jax.experimental import pallas as pl
from jax.experimental.pallas import tpu as pltpu
from jax.sharding import PartitionSpec as P

MESH = pl.DeviceIdType.MESH
F32 = jnp.float32
BF16 = jnp.bfloat16


def split_two(value):
    high = value.astype(BF16)
    low = (value - high.astype(F32)).astype(BF16)
    return high, low


def iota(shape, dim):
    return lax.broadcasted_iota(jnp.int32, shape, dim)


def kernel(
    dims,
    x_hbm,
    w_hbm,
    down_hbm,
    up_hbm,
    ra_col,
    ra_row,
    ap_col,
    ap_row,
    out,
    x,
    w,
    down,
    up,
    send,
    recv,
    flipped,
    lab_send,
    lab_recv,
    red,
    upd_send,
    upd_recv,
    part,
    rs_recv,
    x_sem,
    load_sem,
    own_sem,
    lab_ssem,
    lab_rsem,
    in_ssem,
    in_rsem,
    red_ssem,
    red_rsem,
    upd_ssem,
    upd_rsem,
    rs_ssem,
    rs_rsem,
):
    reps, tps, steps, rows, cap, grouped, rank = dims
    slots = reps * cap
    width = x.shape[1]
    cols = out.shape[1]
    me = lax.axis_index("rep")
    mt = lax.axis_index("tp")

    def others(count, mine, fn):
        def body(k, carry):
            fn(lax.rem(mine + k, count))
            return carry

        lax.fori_loop(1, count, body, 0)

    def over(count, fn):
        def body(k, carry):
            fn(k)
            return carry

        lax.fori_loop(0, count, body, 0)

    x_loads = [
        pltpu.make_async_copy(
            x_hbm.at[pl.ds(s * rows, rows)], x.at[pl.ds(s * rows, rows)], x_sem.at[s]
        )
        for s in range(steps)
    ]
    for load in x_loads:
        load.start()
    w_load = pltpu.make_async_copy(w_hbm, w, load_sem.at[0])
    down_load = pltpu.make_async_copy(down_hbm, down, load_sem.at[1])
    up_load = pltpu.make_async_copy(up_hbm, up, load_sem.at[2])
    w_load.start()
    down_load.start()
    up_load.start()

    barrier = pltpu.get_barrier_semaphore()
    others(
        reps,
        me,
        lambda d: pl.semaphore_signal(barrier, inc=1, device_id={"rep": d}, device_id_type=MESH),
    )
    others(
        tps,
        mt,
        lambda t: pl.semaphore_signal(barrier, inc=1, device_id={"tp": t}, device_id_type=MESH),
    )

    adapters = ap_row.shape[1]
    pos_col = jnp.sum(
        jnp.where(ra_col[...] == iota((rows, adapters), 1), ap_row[...], 0), axis=1, keepdims=True
    )
    pos_row = jnp.sum(
        jnp.where(ra_row[...] == iota((adapters, rows), 0), ap_col[...], 0), axis=0, keepdims=True
    )
    own_col, own_row = lax.div(pos_col, grouped), lax.div(pos_row, grouped)
    same = own_col == own_row
    sub, lane = iota((rows, rows), 0), iota((rows, rows), 1)
    rank_col = jnp.sum(jnp.where(same & (lane < sub), 1, 0), axis=1, keepdims=True)
    rank_row = jnp.sum(jnp.where(same & (sub < lane), 1, 0), axis=0, keepdims=True)
    target_col = own_col * cap + rank_col
    target_row = own_row * cap + rank_row
    landing = target_row == iota((slots, rows), 0)
    pick = jnp.where(landing, 1.0, 0.0).astype(BF16)
    within = pos_row - own_row * grouped
    label = jnp.sum(jnp.where(landing, within + 1, 0), axis=1, keepdims=True) - 1
    lab_send[...] = jnp.broadcast_to(label, (slots, 128)).astype(F32).reshape(reps, cap, 128)

    pl.semaphore_wait(barrier, reps + tps - 2)

    def lab_copy(there, src):
        return pltpu.make_async_remote_copy(
            src_ref=lab_send.at[there],
            dst_ref=lab_recv.at[src],
            send_sem=lab_ssem.at[there],
            recv_sem=lab_rsem.at[src],
            device_id={"rep": there},
            device_id_type=MESH,
        )

    def in_copy(s, there, src):
        return pltpu.make_async_remote_copy(
            src_ref=send.at[s, there],
            dst_ref=recv.at[s, src],
            send_sem=in_ssem.at[s, there],
            recv_sem=in_rsem.at[s, src],
            device_id={"rep": there},
            device_id_type=MESH,
        )

    def own_copy(s):
        return pltpu.make_async_copy(send.at[s, me], recv.at[s, me], own_sem.at[s])

    def red_copy(s, there, src):
        return pltpu.make_async_remote_copy(
            src_ref=red.at[s, mt],
            dst_ref=red.at[s, src],
            send_sem=red_ssem.at[s, there],
            recv_sem=red_rsem.at[s, src],
            device_id={"tp": there},
            device_id_type=MESH,
        )

    def upd_copy(s, there, src):
        return pltpu.make_async_remote_copy(
            src_ref=upd_send.at[s, there],
            dst_ref=upd_recv.at[s, src],
            send_sem=upd_ssem.at[s, there],
            recv_sem=upd_rsem.at[s, src],
            device_id={"rep": there},
            device_id_type=MESH,
        )

    def rs_copy(there, src):
        return pltpu.make_async_remote_copy(
            src_ref=part.at[there],
            dst_ref=rs_recv.at[src],
            send_sem=rs_ssem.at[there],
            recv_sem=rs_rsem.at[src],
            device_id={"tp": there},
            device_id_type=MESH,
        )

    others(reps, me, lambda d: lab_copy(d, me).start())
    lab_own = pltpu.make_async_copy(lab_send.at[me], lab_recv.at[me], load_sem.at[3])
    lab_own.start()
    chunk = 512
    for s in range(steps):
        x_loads[s].wait()

        def place(c, s=s):
            at = pl.ds(pl.multiple_of(c * chunk, chunk), chunk)
            piece = jnp.dot(
                pick, x[s * rows : (s + 1) * rows, at], preferred_element_type=F32
            )
            send[s, :, :, at] = piece.astype(BF16).reshape(reps, cap, chunk)

        over(width // chunk, place)
        others(reps, me, lambda d, s=s: in_copy(s, d, me).start())
        own_copy(s).start()

    w_load.wait()

    def base_block(t):
        at = pl.ds(pl.multiple_of(t * cols, cols), cols)
        part[t] = jnp.dot(x[...], w[:, at], preferred_element_type=F32)

    def base_send(t):
        base_block(t)
        rs_copy(t, mt).start()

    others(tps, mt, base_send)
    base_block(mt)

    down_load.wait()
    up_load.wait()
    lab_own.wait()
    others(reps, me, lambda d: lab_copy(me, d).wait_recv())
    lab_flat = lab_recv[...].reshape(slots, 128)
    lab_row = jnp.transpose(lab_flat)[0:1, :].astype(jnp.int32)
    lab_col = lab_flat[:, 0:1].astype(jnp.int32)

    block = min(8, grouped)
    wide = max(1, 256 // rank)
    wide = min(wide, grouped)

    def step(s):
        own_copy(s).wait()
        others(reps, me, lambda d: in_copy(s, me, d).wait_recv())
        flipped[...] = jnp.transpose(recv[s].reshape(slots, width))

        def shrink_block(b, acc):
            at = pl.ds(pl.multiple_of(b * block * rank, block * rank), block * rank)
            y = jnp.dot(down[at, :], flipped[...], preferred_element_type=F32)
            for i in range(block):
                acc = jnp.where(
                    lab_row == b * block + i, y[i * rank : (i + 1) * rank, :], acc
                )
            return acc

        red[s, mt] = lax.fori_loop(
            0, grouped // block, shrink_block, jnp.zeros((rank, slots), F32)
        )
        others(tps, mt, lambda t: red_copy(s, t, mt).start())
        others(tps, mt, lambda t: red_copy(s, mt, t).wait_recv())
        total = red[s, 0]
        for t in range(1, tps):
            total = total + red[s, t]
        mine = jnp.transpose(total)
        high = mine.astype(BF16).astype(F32)
        low = mine - high
        high = jnp.concatenate([high] * wide, axis=1)
        low = jnp.concatenate([low] * wide, axis=1)
        group = lax.div(iota((slots, wide * rank), 1), rank)

        def expand_block(g, acc):
            at = pl.ds(pl.multiple_of(g * wide * rank, wide * rank), wide * rank)
            here = (lab_col - g * wide) == group
            some = up[at, :]
            acc = acc + jnp.dot(
                jnp.where(here, high, 0.0).astype(BF16), some, preferred_element_type=F32
            )
            return acc + jnp.dot(
                jnp.where(here, low, 0.0).astype(BF16), some, preferred_element_type=F32
            )

        updates = lax.fori_loop(
            0, grouped // wide, expand_block, jnp.zeros((slots, cols), F32)
        )
        upd_send[s] = updates.reshape(reps, cap, cols)
        upd_recv[s, me] = upd_send[s, me]
        others(reps, me, lambda d: upd_copy(s, d, me).start())

    over(steps, step)

    others(tps, mt, lambda t: rs_copy(mt, t).wait_recv())
    take = jnp.where(target_col == iota((rows, slots), 1), 1.0, 0.0).astype(BF16)

    def finish(s):
        at = pl.ds(pl.multiple_of(s * rows, rows), rows)
        total = part[mt, at, :]

        def add(k, total):
            return total + rs_recv[lax.rem(mt + k, tps), at, :]

        total = lax.fori_loop(1, tps, add, total)
        others(reps, me, lambda d: upd_copy(s, me, d).wait_recv())
        high, low = split_two(upd_recv[s].reshape(slots, cols))
        deltas = jnp.dot(take, high, preferred_element_type=F32) + jnp.dot(
            take, low, preferred_element_type=F32
        )
        out[at, :] = (total + deltas).astype(BF16)

    over(steps, finish)

    others(reps, me, lambda d: lab_copy(d, me).wait_send())
    others(tps, mt, lambda t: rs_copy(t, mt).wait_send())

    def drain(s):
        others(reps, me, lambda d: in_copy(s, d, me).wait_send())
        others(tps, mt, lambda t: red_copy(s, t, mt).wait_send())
        others(reps, me, lambda d: upd_copy(s, d, me).wait_send())

    over(steps, drain)


def local(x, w, down, up, request_adapter, adapter_position):
    steps, rows, width = x.shape
    reps, tps = lax.axis_size("rep"), lax.axis_size("tp")
    grouped, rank, _ = down.shape
    cols = up.shape[2]
    cap = -(-(2 * rows // reps) // 16) * 16
    slots = reps * cap
    adapters = adapter_position.shape[0]
    any_spec = pl.BlockSpec(memory_space=pl.ANY)
    vmem_spec = pl.BlockSpec(memory_space=pltpu.VMEM)
    dma = pltpu.SemaphoreType.DMA
    dims = (reps, tps, steps, rows, cap, grouped, rank)
    keys = pl.pallas_call(
        functools.partial(kernel, dims),
        out_shape=jax.ShapeDtypeStruct((steps * rows, cols), BF16),
        in_specs=[any_spec] * 4 + [vmem_spec] * 4,
        out_specs=vmem_spec,
        scratch_shapes=[
            pltpu.VMEM((steps * rows, width), BF16),
            pltpu.VMEM(w.shape, BF16),
            pltpu.VMEM((grouped * rank, width), BF16),
            pltpu.VMEM((grouped * rank, cols), BF16),
            pltpu.VMEM((steps, reps, cap, width), BF16),
            pltpu.VMEM((steps, reps, cap, width), BF16),
            pltpu.VMEM((width, slots), BF16),
            pltpu.VMEM((reps, cap, 128), F32),
            pltpu.VMEM((reps, cap, 128), F32),
            pltpu.VMEM((steps, tps, rank, slots), F32),
            pltpu.VMEM((steps, reps, cap, cols), F32),
            pltpu.VMEM((steps, reps, cap, cols), F32),
            pltpu.VMEM((tps, steps * rows, cols), F32),
            pltpu.VMEM((tps, steps * rows, cols), F32),
            dma((steps,)),
            dma((4,)),
            dma((steps,)),
            dma((reps,)),
            dma((reps,)),
            dma((steps, reps)),
            dma((steps, reps)),
            dma((steps, tps)),
            dma((steps, tps)),
            dma((steps, reps)),
            dma((steps, reps)),
            dma((tps,)),
            dma((tps,)),
        ],
        compiler_params=pltpu.CompilerParams(
            collective_id=0, has_side_effects=True, vmem_limit_bytes=62 * 1024 * 1024
        ),
        cost_estimate=pl.CostEstimate(
            flops=2 * steps * slots * grouped * rank * width,
            bytes_accessed=2 * grouped * rank * width,
            transcendentals=0,
        ),
    )(
        x.reshape(steps * rows, width),
        w,
        down.reshape(grouped * rank, width),
        up.reshape(grouped * rank, cols),
        request_adapter.reshape(rows, 1),
        request_adapter.reshape(1, rows),
        adapter_position.reshape(adapters, 1),
        adapter_position.reshape(1, adapters),
    )
    return keys.reshape(steps, rows, cols)


def solution(mesh):
    return jax.shard_map(
        local,
        mesh=mesh,
        in_specs=(
            P(None, ("dom", "rep"), "tp"),
            P("tp", None),
            P("rep", None, "tp"),
            P("rep", None, "tp"),
            P(("dom", "rep")),
            P("dom"),
        ),
        out_specs=P(None, ("dom", "rep"), "tp"),
        check_vma=False,
    )
```

```python
import functools

import jax
import jax.numpy as jnp
from jax import lax
from jax.experimental import pallas as pl
from jax.experimental.pallas import tpu as pltpu
from jax.sharding import PartitionSpec as P

MESH = pl.DeviceIdType.MESH
F32 = jnp.float32
BF16 = jnp.bfloat16


def split_two(value):
    high = value.astype(BF16)
    low = (value - high.astype(F32)).astype(BF16)
    return high, low


def iota(shape, dim):
    return lax.broadcasted_iota(jnp.int32, shape, dim)


def kernel(
    dims,
    x_hbm,
    w_hbm,
    down_hbm,
    up_hbm,
    ra_row,
    ap_row,
    out,
    x,
    w,
    down,
    up,
    send,
    recv,
    flipped,
    lab_send,
    lab_recv,
    lab_rows,
    red,
    upd_send,
    upd_recv,
    part,
    rs_recv,
    x_sem,
    load_sem,
    own_sem,
    lab_ssem,
    lab_rsem,
    in_ssem,
    in_rsem,
    red_ssem,
    red_rsem,
    upd_ssem,
    upd_rsem,
    rs_ssem,
    rs_rsem,
):
    reps, tps, steps, rows, cap, halves, grouped, rank = dims
    hcap = cap // halves
    slots = reps * hcap
    chunks = steps * halves
    width = x.shape[1]
    cols = out.shape[1]
    me = lax.axis_index("rep")
    mt = lax.axis_index("tp")

    def others(count, mine, fn):
        def body(k, carry):
            fn(lax.rem(mine + k, count))
            return carry

        lax.fori_loop(1, count, body, 0)

    def over(count, fn):
        def body(k, carry):
            fn(k)
            return carry

        lax.fori_loop(0, count, body, 0)

    x_loads = [
        pltpu.make_async_copy(
            x_hbm.at[pl.ds(s * rows, rows)], x.at[pl.ds(s * rows, rows)], x_sem.at[s]
        )
        for s in range(steps)
    ]
    for load in x_loads:
        load.start()
    w_load = pltpu.make_async_copy(w_hbm, w, load_sem.at[0])
    down_load = pltpu.make_async_copy(down_hbm, down, load_sem.at[1])
    up_load = pltpu.make_async_copy(up_hbm, up, load_sem.at[2])
    w_load.start()
    down_load.start()
    up_load.start()

    barrier = pltpu.get_barrier_semaphore()
    others(
        reps,
        me,
        lambda d: pl.semaphore_signal(barrier, inc=1, device_id={"rep": d}, device_id_type=MESH),
    )
    others(
        tps,
        mt,
        lambda t: pl.semaphore_signal(barrier, inc=1, device_id={"tp": t}, device_id_type=MESH),
    )

    adapters = ap_row.shape[1]

    def column(row):
        n = row.shape[1]
        return jnp.sum(
            jnp.where(iota((n, n), 0) == iota((n, n), 1), row, 0), axis=1, keepdims=True
        )

    ap_col = column(ap_row[...])
    pos_row = jnp.sum(
        jnp.where(ra_row[...] == iota((adapters, rows), 0), ap_col, 0), axis=0, keepdims=True
    )
    pos_col = column(pos_row)
    own_col, own_row = lax.div(pos_col, grouped), lax.div(pos_row, grouped)
    same = own_col == own_row
    sub, lane = iota((rows, rows), 0), iota((rows, rows), 1)
    rank_col = jnp.sum(jnp.where(same & (lane < sub), 1, 0), axis=1, keepdims=True)
    rank_row = jnp.sum(jnp.where(same & (sub < lane), 1, 0), axis=0, keepdims=True)
    half_col, half_row = lax.div(rank_col, hcap), lax.div(rank_row, hcap)
    target_col = half_col * slots + own_col * hcap + (rank_col - half_col * hcap)
    target_row = half_row * slots + own_row * hcap + (rank_row - half_row * hcap)
    landing = target_row == iota((halves * slots, rows), 0)
    pick = jnp.where(landing, 1.0, 0.0).astype(BF16)
    within = pos_row - own_row * grouped
    label = jnp.sum(jnp.where(landing, within + 1, 0), axis=1, keepdims=True) - 1
    lab_send[...] = jnp.broadcast_to(label.astype(F32), (halves * slots, 128)).reshape(
        halves, reps, hcap, 128
    )

    pl.semaphore_wait(barrier, reps + tps - 2)

    def lab_copy(h, there, src):
        return pltpu.make_async_remote_copy(
            src_ref=lab_send.at[h, there],
            dst_ref=lab_recv.at[h, src],
            send_sem=lab_ssem.at[h, there],
            recv_sem=lab_rsem.at[h, src],
            device_id={"rep": there},
            device_id_type=MESH,
        )

    def in_copy(s, there, src):
        return pltpu.make_async_remote_copy(
            src_ref=send.at[s, there],
            dst_ref=recv.at[s, src],
            send_sem=in_ssem.at[s, there],
            recv_sem=in_rsem.at[s, src],
            device_id={"rep": there},
            device_id_type=MESH,
        )

    def own_copy(s):
        return pltpu.make_async_copy(send.at[s, me], recv.at[s, me], own_sem.at[s])

    def red_copy(s, there, src):
        return pltpu.make_async_remote_copy(
            src_ref=red.at[s, mt],
            dst_ref=red.at[s, src],
            send_sem=red_ssem.at[s, there],
            recv_sem=red_rsem.at[s, src],
            device_id={"tp": there},
            device_id_type=MESH,
        )

    def upd_copy(s, there, src):
        return pltpu.make_async_remote_copy(
            src_ref=upd_send.at[s, there],
            dst_ref=upd_recv.at[s, src],
            send_sem=upd_ssem.at[s, there],
            recv_sem=upd_rsem.at[s, src],
            device_id={"rep": there},
            device_id_type=MESH,
        )

    def rs_copy(there, src):
        return pltpu.make_async_remote_copy(
            src_ref=part.at[there],
            dst_ref=rs_recv.at[src],
            send_sem=rs_ssem.at[there],
            recv_sem=rs_rsem.at[src],
            device_id={"tp": there},
            device_id_type=MESH,
        )

    for h in range(halves):
        others(reps, me, lambda d, h=h: lab_copy(h, d, me).start())
        lab_recv[h, me] = lab_send[h, me]
    chunk = 512
    for s in range(steps):
        x_loads[s].wait()

        for h in range(halves):

            def place(c, s=s, h=h):
                at = pl.ds(pl.multiple_of(c * chunk, chunk), chunk)
                piece = jnp.dot(
                    pick[h * slots : (h + 1) * slots],
                    x[s * rows : (s + 1) * rows, at],
                    preferred_element_type=F32,
                )
                send[s * halves + h, :, :, at] = piece.astype(BF16).reshape(reps, hcap, chunk)

            over(width // chunk, place)
            others(reps, me, lambda d, q=s * halves + h: in_copy(q, d, me).start())
            own_copy(s * halves + h).start()

    w_load.wait()

    def base_block(t):
        at = pl.ds(pl.multiple_of(t * cols, cols), cols)
        part[t] = jnp.dot(x[...], w[:, at], preferred_element_type=F32)

    def base_send(t):
        base_block(t)
        rs_copy(t, mt).start()

    others(tps, mt, base_send)
    base_block(mt)

    down_load.wait()
    up_load.wait()
    for h in range(halves):
        others(reps, me, lambda d, h=h: lab_copy(h, me, d).wait_recv())
        flat = lab_recv[h].reshape(slots, 128)
        lab_rows[h] = jnp.transpose(flat)[0:8, :].astype(jnp.int32)

    block = min(8, grouped)
    wide = max(1, 256 // rank)
    wide = min(wide, grouped)

    def step(s):
        h = lax.rem(s, halves)
        lab_row = lab_rows[h][0:1, :]
        lab_col = lab_recv[h].reshape(slots, 128)[:, 0:1].astype(jnp.int32)
        own_copy(s).wait()
        others(reps, me, lambda d: in_copy(s, me, d).wait_recv())
        flipped[...] = jnp.transpose(recv[s].reshape(slots, width))

        def shrink_block(b, acc):
            at = pl.ds(pl.multiple_of(b * block * rank, block * rank), block * rank)
            y = jnp.dot(down[at, :], flipped[...], preferred_element_type=F32)
            for i in range(block):
                acc = jnp.where(
                    lab_row == b * block + i, y[i * rank : (i + 1) * rank, :], acc
                )
            return acc

        red[s, mt] = lax.fori_loop(
            0, grouped // block, shrink_block, jnp.zeros((rank, slots), F32)
        )
        others(tps, mt, lambda t: red_copy(s, t, mt).start())
        others(tps, mt, lambda t: red_copy(s, mt, t).wait_recv())
        total = red[s, 0]
        for t in range(1, tps):
            total = total + red[s, t]
        mine = jnp.transpose(total)
        high = mine.astype(BF16).astype(F32)
        low = mine - high
        high = jnp.concatenate([high] * wide, axis=1)
        low = jnp.concatenate([low] * wide, axis=1)
        group = lax.div(iota((slots, wide * rank), 1), rank)

        def expand_block(g, acc):
            at = pl.ds(pl.multiple_of(g * wide * rank, wide * rank), wide * rank)
            here = (lab_col - g * wide) == group
            some = up[at, :]
            acc = acc + jnp.dot(
                jnp.where(here, high, 0.0).astype(BF16), some, preferred_element_type=F32
            )
            return acc + jnp.dot(
                jnp.where(here, low, 0.0).astype(BF16), some, preferred_element_type=F32
            )

        updates = lax.fori_loop(
            0, grouped // wide, expand_block, jnp.zeros((slots, cols), F32)
        )
        upd_send[s] = updates.reshape(reps, hcap, cols)
        upd_recv[s, me] = upd_send[s, me]
        others(reps, me, lambda d: upd_copy(s, d, me).start())

    over(chunks, step)

    others(tps, mt, lambda t: rs_copy(mt, t).wait_recv())
    take = jnp.where(target_col == iota((rows, halves * slots), 1), 1.0, 0.0).astype(BF16)

    def finish(s):
        at = pl.ds(pl.multiple_of(s * rows, rows), rows)
        total = part[mt, at, :]

        def add(k, total):
            return total + rs_recv[lax.rem(mt + k, tps), at, :]

        total = lax.fori_loop(1, tps, add, total)
        for h in range(halves):
            q = s * halves + h
            others(reps, me, lambda d, q=q: upd_copy(q, me, d).wait_recv())
            high, low = split_two(upd_recv[q].reshape(slots, cols))
            mine = take[:, h * slots : (h + 1) * slots]
            total = total + jnp.dot(mine, high, preferred_element_type=F32)
            total = total + jnp.dot(mine, low, preferred_element_type=F32)
        out[at, :] = total.astype(BF16)

    over(steps, finish)

    for h in range(halves):
        others(reps, me, lambda d, h=h: lab_copy(h, d, me).wait_send())
    others(tps, mt, lambda t: rs_copy(t, mt).wait_send())

    def drain(s):
        others(reps, me, lambda d: in_copy(s, d, me).wait_send())
        others(tps, mt, lambda t: red_copy(s, t, mt).wait_send())
        others(reps, me, lambda d: upd_copy(s, d, me).wait_send())

    over(chunks, drain)


def local(x, w, down, up, request_adapter, adapter_position):
    steps, rows, width = x.shape
    reps, tps = lax.axis_size("rep"), lax.axis_size("tp")
    grouped, rank, _ = down.shape
    cols = up.shape[2]
    cap = -(-(2 * rows // reps) // 16) * 16
    halves = 2 if cap % 32 == 0 else 1
    hcap = cap // halves
    slots = reps * hcap
    chunks = steps * halves
    adapters = adapter_position.shape[0]
    any_spec = pl.BlockSpec(memory_space=pl.ANY)
    vmem_spec = pl.BlockSpec(memory_space=pltpu.VMEM)
    dma = pltpu.SemaphoreType.DMA
    dims = (reps, tps, steps, rows, cap, halves, grouped, rank)
    keys = pl.pallas_call(
        functools.partial(kernel, dims),
        out_shape=jax.ShapeDtypeStruct((steps * rows, cols), BF16),
        in_specs=[any_spec] * 4 + [vmem_spec] * 2,
        out_specs=vmem_spec,
        scratch_shapes=[
            pltpu.VMEM((steps * rows, width), BF16),
            pltpu.VMEM(w.shape, BF16),
            pltpu.VMEM((grouped * rank, width), BF16),
            pltpu.VMEM((grouped * rank, cols), BF16),
            pltpu.VMEM((chunks, reps, hcap, width), BF16),
            pltpu.VMEM((chunks, reps, hcap, width), BF16),
            pltpu.VMEM((width, slots), BF16),
            pltpu.VMEM((halves, reps, hcap, 128), F32),
            pltpu.VMEM((halves, reps, hcap, 128), F32),
            pltpu.VMEM((halves, 8, slots), jnp.int32),
            pltpu.VMEM((chunks, tps, rank, slots), F32),
            pltpu.VMEM((chunks, reps, hcap, cols), F32),
            pltpu.VMEM((chunks, reps, hcap, cols), F32),
            pltpu.VMEM((tps, steps * rows, cols), F32),
            pltpu.VMEM((tps, steps * rows, cols), F32),
            dma((steps,)),
            dma((3,)),
            dma((chunks,)),
            dma((halves, reps)),
            dma((halves, reps)),
            dma((chunks, reps)),
            dma((chunks, reps)),
            dma((chunks, tps)),
            dma((chunks, tps)),
            dma((chunks, reps)),
            dma((chunks, reps)),
            dma((tps,)),
            dma((tps,)),
        ],
        compiler_params=pltpu.CompilerParams(
            collective_id=0, has_side_effects=True, vmem_limit_bytes=62 * 1024 * 1024
        ),
        cost_estimate=pl.CostEstimate(
            flops=2 * chunks * slots * grouped * rank * width,
            bytes_accessed=2 * grouped * rank * width,
            transcendentals=0,
        ),
    )(
        x.reshape(steps * rows, width),
        w,
        down.reshape(grouped * rank, width),
        up.reshape(grouped * rank, cols),
        request_adapter.reshape(1, rows),
        adapter_position.reshape(1, adapters),
    )
    return keys.reshape(steps, rows, cols)


def solution(mesh):
    return jax.shard_map(
        local,
        mesh=mesh,
        in_specs=(
            P(None, ("dom", "rep"), "tp"),
            P("tp", None),
            P("rep", None, "tp"),
            P("rep", None, "tp"),
            P(("dom", "rep")),
            P("dom"),
        ),
        out_specs=P(None, ("dom", "rep"), "tp"),
        check_vma=False,
    )
```
